32 devices in a mesh: pix: 4 (over x, core), ch: 8 (over z, y).
Axes of the slice: x: 2, y: 2, z: 4, core: 2. Of those that a mesh axis runs over, the one named last changes fastest.
Arguments:
- image_in: bfloat16 [128, 1024, 128], P('pix', 'ch'), may hold values from -6 to 6
- pre_act: bfloat16 [64, 64, 2048], P('pix', None, 'ch'), may hold values from -8 to 8
- grad_out: bfloat16 [64, 64, 2048], P('pix', None, 'ch'), may hold values from -6 to 6
- conv_weight: bfloat16 [3, 3, 1024, 2048], P(None, None, 'ch', 'pix'), may hold values from -0.0625 to 0.0625
- mix_weight: bfloat16 [32, 64, 64], P('ch'), may hold values from -0.75 to 0.75
Outputs:
- grad_in: bfloat16 [128, 1024, 128], P('pix', 'ch')
- grad_conv: float32 [3, 3, 1024, 2048], P(None, None, 'ch', 'pix')
- grad_mix: float32 [32, 64, 64], P('ch')
The draws below stay inside these ranges and needn't reach their ends.
All inputs are finite; a program needn't handle non-finite values.
Results may differ from the reference program's by a relative error of at most 0.0049.
Values may be sent and summed in bfloat16 or wider, within the bound.
No kernel may reach another device: no remote copies, remote signals or barrier semaphores. Data moves between devices by JAX's collectives and lax.ppermute only.
A program may use at most 128 MiB of HBM per device.

```python
import jax
import jax.numpy as jnp
from jax import lax

CIN = 1024
COUT = 2048
GROUPS = 32
ROWS_DEV = 16
WIDTH_OUT = 64
GROUP_WIDTH = 64
HEIGHT_OUT = 64
WIDTH_IN = 128
ROWS = 64
N_PIX = 4


def block_levels(rng, dims, pieces, least, high):
    def one(position, shards_of):
        draws = jax.random.uniform(jax.random.fold_in(jax.random.fold_in(rng, 6), position), (shards_of,), jnp.float32, least / len(pieces), high / len(pieces))
        return jnp.repeat(jnp.exp(draws), dims[position] // shards_of).reshape((-1,) + (1,) * (len(dims) - position - 1))

    gain = one(*pieces[0])
    for cut in pieces[1:]:
        gain = gain * one(*cut)
    return gain


def scatter_about(rng, dims, spread, limit, cuts=(), kind=jnp.bfloat16):
    drawn = spread * jax.random.normal(rng, dims, jnp.float32)
    if cuts:
        drawn = drawn * block_levels(rng, dims, cuts, -0.22, 0.18)
    return jnp.clip(drawn, -limit, limit).astype(kind)


def setup_inputs(seed: int = 0) -> dict:
    keys = jax.random.split(jax.random.key(seed), 6)
    image_in = scatter_about(keys[0], (2 * ROWS, CIN, WIDTH_IN), 1.0, 6.0, ((0, 4), (1, 8)))
    pre_act = scatter_about(keys[1], (ROWS, WIDTH_OUT, COUT), 1.5, 8.0, ((0, 4), (2, 8)))
    grad_out = scatter_about(keys[2], (ROWS, WIDTH_OUT, COUT), 1.0, 6.0, ((0, 4), (2, 8)))
    conv_weight = scatter_about(keys[3], (3, 3, CIN, COUT), (9 * CIN) ** -0.5, 0.0625, ((2, 8), (3, 4)))
    mix_weight = scatter_about(keys[4], (GROUPS, GROUP_WIDTH, GROUP_WIDTH), GROUP_WIDTH ** -0.5, 0.75, ((0, 8),))
    return dict(image_in=image_in, pre_act=pre_act, grad_out=grad_out, conv_weight=conv_weight, mix_weight=mix_weight)


def matmul_high(left, right):
    return jnp.dot(left, right, preferred_element_type=jnp.float32, precision=lax.Precision.HIGHEST)

def select_cols_in(values, col_tap):
    if col_tap == 0:
        zero_col = jnp.zeros(values[:, :, :1, 1].shape, values.dtype)
        return jnp.concatenate([zero_col, values[:, :, :-1, 1]], axis=2)
    return values[:, :, :, col_tap - 1]

def select_cols_grad(values, col_tap):
    if col_tap == 0:
        zero_col = jnp.zeros(values[:, :, :1].shape, values.dtype)
        return jnp.concatenate([values[:, :, 1:], zero_col], axis=2)
    return values

def reference(image_in, pre_act, grad_out, conv_weight, mix_weight):
    rows = ROWS_DEV * N_PIX
    images = rows // HEIGHT_OUT
    pixels = rows * WIDTH_OUT
    scale = 1.0 / float(pixels) ** 0.5
    pre_f = pre_act.astype(jnp.float32)
    sigmoid_h = jax.nn.sigmoid(pre_f)
    act = (pre_f * sigmoid_h).astype(jnp.bfloat16)
    grad_groups = grad_out.astype(jnp.float32).reshape(rows, WIDTH_OUT, GROUPS, GROUP_WIDTH)
    mix_f = mix_weight.astype(jnp.float32)
    grad_act = jnp.einsum('rwgi,gji->rwgj', grad_groups, mix_f, precision=lax.Precision.HIGHEST).reshape(rows, WIDTH_OUT, COUT)
    grad_pre = (grad_act * (sigmoid_h * (1.0 + pre_f * (1.0 - sigmoid_h)))).astype(jnp.bfloat16)
    act_groups = act.astype(jnp.float32).reshape(rows, WIDTH_OUT, GROUPS, GROUP_WIDTH)
    grad_mix = jnp.einsum('rwgj,rwgi->gji', act_groups, grad_groups, precision=lax.Precision.HIGHEST) * scale
    phases = jnp.transpose(image_in.astype(jnp.float32).reshape(images, HEIGHT_OUT, 2, CIN, WIDTH_OUT, 2), (0, 1, 2, 4, 5, 3))
    zero_row = jnp.zeros((images, 1, WIDTH_OUT, 2, CIN), jnp.float32)
    odd_prev = jnp.concatenate([zero_row, phases[:, :-1, 1]], axis=1)
    row_sources = [odd_prev, phases[:, :, 0], phases[:, :, 1]]
    grad_flat = grad_pre.astype(jnp.float32).reshape(pixels, COUT)
    conv_f = conv_weight.astype(jnp.float32)
    tap_grads = []
    for row_tap in range(3):
        line = []
        for col_tap in range(3):
            taps = select_cols_in(row_sources[row_tap], col_tap).reshape(pixels, CIN)
            line.append(matmul_high(taps.T, grad_flat))
        tap_grads.append(jnp.stack(line))
    grad_conv = jnp.stack(tap_grads) * scale
    grad_img = grad_pre.astype(jnp.float32).reshape(images, HEIGHT_OUT, WIDTH_OUT, COUT)
    zero_grad = jnp.zeros((images, 1, WIDTH_OUT, COUT), jnp.float32)
    grad_up = jnp.concatenate([grad_img[:, 1:], zero_grad], axis=1)

    def term(source, row_tap, col_tap):
        shifted = select_cols_grad(source, col_tap).reshape(pixels, COUT)
        return matmul_high(shifted, conv_f[row_tap, col_tap].T)
    even_even = term(grad_img, 1, 1)
    even_odd = term(grad_img, 1, 2) + term(grad_img, 1, 0)
    odd_even = term(grad_img, 2, 1) + term(grad_up, 0, 1)
    odd_odd = term(grad_img, 2, 2) + term(grad_img, 2, 0) + term(grad_up, 0, 2) + term(grad_up, 0, 0)
    stacked = jnp.stack([even_even, even_odd, odd_even, odd_odd]).reshape(2, 2, images, HEIGHT_OUT, WIDTH_OUT, CIN)
    grad_in = jnp.transpose(stacked, (2, 3, 0, 5, 4, 1)).reshape(2 * rows, CIN, 2 * WIDTH_OUT).astype(jnp.bfloat16)
    return (grad_in, grad_conv, grad_mix)
```

```python
import functools

import jax
import jax.numpy as jnp
from jax import lax
from jax.experimental import pallas as pl
from jax.experimental.pallas import tpu as pltpu
from jax.sharding import PartitionSpec as P

TILES = 4
GROUP_WIDTH = 64
BF = jnp.bfloat16
F32 = jnp.float32
VMEM_LIMIT = 56 * 2**20


def params():
    return pltpu.CompilerParams(vmem_limit_bytes=VMEM_LIMIT)


def dot_nn(a, b):
    return lax.dot_general(a, b, (((1,), (0,)), ((), ())), preferred_element_type=F32)


def dot_nt(a, b):
    return lax.dot_general(a, b, (((1,), (1,)), ((), ())), preferred_element_type=F32)


def dot_tn(a, b):
    return lax.dot_general(a, b, (((0,), (0,)), ((), ())), preferred_element_type=F32)


def iota(shape, dim):
    return lax.broadcasted_iota(jnp.int32, shape, dim)


def pre_kernel(grad_ref, pre_ref, mix_ref, out_ref, mix_out_ref):
    chans = grad_ref.shape[1]
    spread = (iota((GROUP_WIDTH, chans), 0) == iota((GROUP_WIDTH, chans), 1) % GROUP_WIDTH).astype(BF)
    same = iota((chans, chans), 0) // GROUP_WIDTH == iota((chans, chans), 1) // GROUP_WIDTH
    blocks = jnp.where(same, dot_nn(mix_ref[...], spread), 0.0).astype(BF)
    grad = grad_ref[...]
    pre = pre_ref[...].astype(F32)
    sig = jax.nn.sigmoid(pre)
    act = (pre * sig).astype(BF)
    grad_act = dot_nt(grad, blocks)
    out_ref[...] = (grad_act * (sig * (1.0 + pre * (1.0 - sig)))).astype(BF)
    full = jnp.where(same, dot_tn(act, grad), 0.0)
    total = full
    for step in range(1, chans // GROUP_WIDTH):
        total = total + pltpu.roll(full, step * GROUP_WIDTH, 1)
    mix_out_ref[...] = total[:, :GROUP_WIDTH]


def pre_gradient(grad_out, pre_act, mix_weight):
    pixels, chans = grad_out.shape
    return pl.pallas_call(
        pre_kernel,
        out_shape=(
            jax.ShapeDtypeStruct((pixels, chans), BF),
            jax.ShapeDtypeStruct((chans, GROUP_WIDTH), F32),
        ),
        compiler_params=params(),
        cost_estimate=pl.CostEstimate(
            flops=4 * pixels * chans * chans, bytes_accessed=6 * pixels * chans, transcendentals=pixels * chans
        ),
        name="pre_grad",
    )(grad_out, pre_act, mix_weight)


def taps_kernel(image_ref, prev_ref, out_ref):
    rows, chans, width = image_ref.shape
    half = width // 2
    col_in = iota((2 * width, 6 * half), 0)
    col_out = iota((2 * width, 6 * half), 1)
    pick = (
        (col_in // width == (col_out % width) // half)
        & (col_in % width == 2 * (col_out % half) + col_out // width - 1)
    ).astype(BF)
    for pair in range(rows // 4):
        for row_tap in range(3):
            first = 4 * pair + row_tap - 1
            upper = prev_ref[...] if first < 0 else image_ref[first]
            both = jnp.concatenate([upper, image_ref[first + 2]], axis=1)
            picked = dot_nn(both, pick).astype(BF)
            for col_tap in range(3):
                tap = 3 * row_tap + col_tap
                out_ref[tap * chans : (tap + 1) * chans, pair * width : (pair + 1) * width] = picked[
                    :, col_tap * width : (col_tap + 1) * width
                ]


def image_taps(image_in, prev_row):
    rows, chans, width = image_in.shape
    pixels = rows * width // 4
    return pl.pallas_call(
        taps_kernel,
        out_shape=jax.ShapeDtypeStruct((9 * chans, pixels), BF),
        compiler_params=params(),
        cost_estimate=pl.CostEstimate(
            flops=rows * chans * width * width * 9 // 2, bytes_accessed=13 * rows * chans * width // 2, transcendentals=0
        ),
        name="taps",
    )(image_in, prev_row)


def image_kernel(
    grad_count, part_count, width, ids_ref, halo_ref, *refs
):
    grads, parts = refs[:grad_count], refs[grad_count : grad_count + part_count]
    out_ref, grad_all, part_all, grad_sem, part_sem = refs[grad_count + part_count :]
    pixels, span = grads[0].shape
    outs, part_span = parts[0].shape
    chans = outs // 9
    tile = 4 * width
    tiles = pixels // tile

    def part_copy(index):
        start = pl.multiple_of(ids_ref[grad_count + index] * part_span, part_span)
        return pltpu.make_async_copy(
            parts[index], part_all.at[:, pl.ds(start, part_span)], part_sem.at[index]
        )

    def grad_copy(index):
        start = pl.multiple_of(ids_ref[index] * span, span)
        return pltpu.make_async_copy(
            grads[index], grad_all.at[:, pl.ds(start, span)], grad_sem.at[index]
        )

    for index in range(part_count):
        part_copy(index).start()
    for index in range(grad_count):
        grad_copy(index).start()

    lane = iota((chans, tile), 1)
    last_col = lane % width == width - 1
    row_end = lane >= tile - width
    place_in = iota((tile, tile), 0)
    place_out = iota((tile, tile), 1)
    place = (
        ((place_in % (2 * width)) // width == place_out // (2 * width))
        & (2 * (place_in % width) + place_in // (2 * width) == place_out % (2 * width))
    ).astype(BF)

    def left(value):
        return jnp.where(last_col, 0.0, pltpu.roll(value, tile - 1, 1))

    def up_terms(terms):
        even, odd = terms[chans : 2 * chans], terms[2 * chans : 3 * chans] + left(terms[:chans])
        return pltpu.roll(even, tile - width, 1), pltpu.roll(odd, tile - width, 1)

    for index in range(part_count):
        part_copy(index).wait()
    for index in range(grad_count):
        grad_copy(index).wait()
    halo = dot_nt(part_all[: 3 * chans], halo_ref[...])
    below = up_terms(jnp.concatenate([halo, jnp.zeros_like(halo)], axis=1))
    for step in reversed(range(tiles)):
        terms = dot_nt(part_all[...], grad_all[step * tile : (step + 1) * tile])
        own = up_terms(terms[: 3 * chans])
        tap = lambda index: terms[index * chans : (index + 1) * chans]
        phases = (
            (tap(4), tap(5) + left(tap(3))),
            (
                tap(7) + jnp.where(row_end, below[0], own[0]),
                tap(8) + left(tap(6)) + jnp.where(row_end, below[1], own[1]),
            ),
        )
        below = own
        for parity in range(2):
            even, odd = (value.astype(BF) for value in phases[parity])
            for pair in range(2):
                cols = slice(pair * 2 * width, (pair + 1) * 2 * width)
                placed = dot_nn(jnp.concatenate([even[:, cols], odd[:, cols]], axis=1), place).astype(BF)
                first = 8 * step + 4 * pair + parity
                out_ref[first] = placed[:, : 2 * width]
                out_ref[first + 2] = placed[:, 2 * width :]


def image_gradient(grads, grad_ids, parts, part_ids, halo, width):
    pixels, span = grads[0].shape
    outs, part_span = parts[0].shape
    full = span * len(grads)
    chans = outs // 9
    ids = jnp.stack([jnp.asarray(value, jnp.int32) for value in (*grad_ids, *part_ids)])
    kernel = functools.partial(image_kernel, len(grads), len(parts), width)
    anywhere = pl.BlockSpec(memory_space=pl.ANY)
    return pl.pallas_call(
        kernel,
        out_shape=jax.ShapeDtypeStruct((2 * pixels // width, chans, 2 * width), BF),
        in_specs=[pl.BlockSpec(memory_space=pltpu.SMEM), pl.BlockSpec(memory_space=pltpu.VMEM)]
        + [anywhere] * (len(grads) + len(parts)),
        out_specs=pl.BlockSpec(memory_space=pltpu.VMEM),
        scratch_shapes=[
            pltpu.VMEM((pixels, full), BF),
            pltpu.VMEM((outs, full), BF),
            pltpu.SemaphoreType.DMA((len(grads),)),
            pltpu.SemaphoreType.DMA((len(parts),)),
        ],
        compiler_params=params(),
        cost_estimate=pl.CostEstimate(
            flops=2 * pixels * outs * full, bytes_accessed=2 * full * (pixels + outs), transcendentals=0
        ),
        name="image_grad",
    )(ids, halo, *grads, *parts)


def step_along(value, axis, steps):
    count = lax.axis_size(axis)
    return lax.ppermute(
        value, axis, [(source, source + steps) for source in range(count) if 0 <= source + steps < count]
    )


def shards(image_in, pre_act, grad_out, conv_weight, mix_weight):
    tile_rows, width, chans = grad_out.shape
    in_chans = image_in.shape[1]
    pix_count, ch_count = lax.axis_size("pix"), lax.axis_size("ch")
    pix_index = lax.axis_index("pix")
    first_tile = pix_index % TILES == 0
    last_tile = pix_index % TILES == TILES - 1
    pixels = tile_rows * width
    scale = 1.0 / float(pix_count * pixels) ** 0.5

    prev_row = step_along(image_in[-1], "pix", 1)
    prev_row = jnp.where(first_tile, jnp.zeros_like(prev_row), prev_row)
    grad_pre, mix_part = pre_gradient(
        grad_out.reshape(pixels, chans),
        pre_act.reshape(pixels, chans),
        mix_weight.reshape(chans, GROUP_WIDTH),
    )
    grad_mix = (lax.psum(mix_part, "pix") * scale).reshape(mix_weight.shape)
    halo = step_along(grad_pre[:width], "pix", -1)
    halo = jnp.where(last_tile, jnp.zeros_like(halo), halo)
    halo_all = lax.all_gather(halo, "ch", axis=1, tiled=True)
    halo_all = jnp.concatenate([halo_all, jnp.zeros_like(halo_all)], axis=0)
    kernel_own = conv_weight.reshape(9 * in_chans, -1)
    taps = image_taps(image_in, prev_row)

    grad_all = lax.all_gather(grad_pre, "ch", axis=0)
    kernel_all = lax.all_gather(kernel_own, "pix", axis=0)
    partial = jnp.concatenate([dot_nn(taps, grad_all[index]).astype(BF) for index in range(ch_count)], axis=1)
    grad_conv = lax.psum_scatter(partial, "pix", scatter_dimension=1, tiled=True).astype(F32) * scale
    grad_in = image_gradient(
        [grad_all[index] for index in range(ch_count)],
        range(ch_count),
        [kernel_all[index] for index in range(pix_count)],
        range(pix_count),
        halo_all,
        width,
    )
    return (grad_in, grad_conv.reshape(conv_weight.shape), grad_mix)


def solution(mesh):
    in_specs = (
        P("pix", "ch", None),
        P("pix", None, "ch"),
        P("pix", None, "ch"),
        P(None, None, "ch", "pix"),
        P("ch", None, None),
    )
    out_specs = (P("pix", "ch", None), P(None, None, "ch", "pix"), P("ch", None, None))
    return jax.shard_map(shards, mesh=mesh, in_specs=in_specs, out_specs=out_specs, check_vma=False)
```

```python
import functools

import jax
import jax.numpy as jnp
from jax import lax
from jax.experimental import pallas as pl
from jax.experimental.pallas import tpu as pltpu
from jax.sharding import PartitionSpec as P

TILES = 4
GROUP_WIDTH = 64
BF = jnp.bfloat16
F32 = jnp.float32
SMALL = pl.CostEstimate(flops=1, bytes_accessed=1, transcendentals=0)


def params(mebibytes):
    return pltpu.CompilerParams(vmem_limit_bytes=mebibytes * 2**20)


def dot_nn(a, b):
    return lax.dot_general(a, b, (((1,), (0,)), ((), ())), preferred_element_type=F32)


def dot_nt(a, b):
    return lax.dot_general(a, b, (((1,), (1,)), ((), ())), preferred_element_type=F32)


def dot_tn(a, b):
    return lax.dot_general(a, b, (((0,), (0,)), ((), ())), preferred_element_type=F32)


def iota(shape, dim):
    return lax.broadcasted_iota(jnp.int32, shape, dim)


def pre_kernel(grad_ref, pre_ref, mix_ref, out_ref, mix_out_ref):
    chans = grad_ref.shape[1]
    spread = (iota((GROUP_WIDTH, chans), 0) == iota((GROUP_WIDTH, chans), 1) % GROUP_WIDTH).astype(BF)
    same = iota((chans, chans), 0) // GROUP_WIDTH == iota((chans, chans), 1) // GROUP_WIDTH
    blocks = jnp.where(same, dot_nn(mix_ref[...], spread), 0.0).astype(BF)
    grad = grad_ref[...]
    pre = pre_ref[...].astype(F32)
    sig = jax.nn.sigmoid(pre)
    act = (pre * sig).astype(BF)
    grad_act = dot_nt(grad, blocks)
    out_ref[...] = (grad_act * (sig * (1.0 + pre * (1.0 - sig)))).astype(BF)
    full = jnp.where(same, dot_tn(act, grad), 0.0)
    total = full
    for step in range(1, chans // GROUP_WIDTH):
        total = total + pltpu.roll(full, step * GROUP_WIDTH, 1)
    mix_out_ref[...] = total[:, :GROUP_WIDTH]


def pre_gradient(grad_out, pre_act, mix_weight):
    pixels, chans = grad_out.shape
    return pl.pallas_call(
        pre_kernel,
        out_shape=(
            jax.ShapeDtypeStruct((pixels, chans), BF),
            jax.ShapeDtypeStruct((chans, GROUP_WIDTH), F32),
        ),
        compiler_params=params(56),
        cost_estimate=SMALL,
        name="pre_grad",
    )(grad_out, pre_act, mix_weight)


def taps_kernel(image_ref, prev_ref, out_ref):
    rows, chans, width = image_ref.shape
    half = width // 2
    col_in = iota((2 * width, 6 * half), 0)
    col_out = iota((2 * width, 6 * half), 1)
    pick = (
        (col_in // width == (col_out % width) // half)
        & (col_in % width == 2 * (col_out % half) + col_out // width - 1)
    ).astype(BF)
    for pair in range(rows // 4):
        for row_tap in range(3):
            first = 4 * pair + row_tap - 1
            upper = prev_ref[...] if first < 0 else image_ref[first]
            both = jnp.concatenate([upper, image_ref[first + 2]], axis=1)
            picked = dot_nn(both, pick).astype(BF)
            for col_tap in range(3):
                tap = 3 * row_tap + col_tap
                out_ref[tap * chans : (tap + 1) * chans, pair * width : (pair + 1) * width] = picked[
                    :, col_tap * width : (col_tap + 1) * width
                ]


def image_taps(image_in, prev_row):
    rows, chans, width = image_in.shape
    pixels = rows * width // 4
    return pl.pallas_call(
        taps_kernel,
        out_shape=jax.ShapeDtypeStruct((9 * chans, pixels), BF),
        compiler_params=params(24),
        cost_estimate=SMALL,
        name="taps",
    )(image_in, prev_row)


def grad_place(place_ref, flips, index):
    if not flips:
        return index
    return ((place_ref[1] + 8 - 2 * (index % 4)) & 7) ^ (index // 4)


def part_place(place_ref, flips, index):
    return place_ref[0] ^ index if flips else index


def image_kernel(
    grad_count, part_count, flips, width, place_ref, halo_ref, *refs
):
    grads, parts = refs[:grad_count], refs[grad_count : grad_count + part_count]
    out_ref, grad_all, part_all, values, grad_sem, part_sem = refs[grad_count + part_count :]
    pixels, span = grads[0].shape
    outs, part_span = parts[0].shape
    chans = outs // 9
    tile = 4 * width
    tiles = pixels // tile

    def part_copy(index):
        start = pl.multiple_of(part_place(place_ref, flips, index) * part_span, part_span)
        return pltpu.make_async_copy(
            parts[index], part_all.at[:, pl.ds(start, part_span)], part_sem.at[index]
        )

    def grad_copy(index, step):
        start = pl.multiple_of(grad_place(place_ref, flips, index) * span, span)
        rows = pl.ds(step * tile, tile)
        return pltpu.make_async_copy(
            grads[index].at[rows], grad_all.at[rows, pl.ds(start, span)], grad_sem.at[index, step]
        )

    for index in range(part_count):
        part_copy(index).start()
    for step in reversed(range(tiles)):
        for index in range(grad_count):
            grad_copy(index, step).start()

    lane = iota((chans, tile), 1)
    last_col = lane % width == width - 1
    row_end = lane >= tile - width
    place_in = iota((tile, tile), 0)
    place_out = iota((tile, tile), 1)
    place = (
        ((place_in % (2 * width)) // width == place_out // (2 * width))
        & (2 * (place_in % width) + place_in // (2 * width) == place_out % (2 * width))
    ).astype(BF)

    def left(value):
        return jnp.where(last_col, 0.0, pltpu.roll(value, tile - 1, 1))

    def up_terms(terms):
        even, odd = terms[chans : 2 * chans], terms[2 * chans : 3 * chans] + left(terms[:chans])
        return pltpu.roll(even, tile - width, 1), pltpu.roll(odd, tile - width, 1)

    for index in range(part_count):
        part_copy(index).wait()
    wide = jnp.concatenate([halo_ref[...]] * 2, axis=1)
    below = (wide[:chans], wide[chans:])
    for step in reversed(range(tiles)):
        for index in range(grad_count):
            grad_copy(index, step).wait()
        terms = dot_nt(part_all[...], grad_all[step * tile : (step + 1) * tile])
        own = up_terms(terms[: 3 * chans])
        tap = lambda index: terms[index * chans : (index + 1) * chans]
        phases = (
            (tap(4), tap(5) + left(tap(3))),
            (
                tap(7) + jnp.where(row_end, below[0], own[0]),
                tap(8) + left(tap(6)) + jnp.where(row_end, below[1], own[1]),
            ),
        )
        below = own
        for parity in range(2):
            even, odd = (value.astype(BF) for value in phases[parity])
            for pair in range(2):
                cols = slice(pair * 2 * width, (pair + 1) * 2 * width)
                rows = slice((2 * parity + pair) * chans, (2 * parity + pair + 1) * chans)
                values[rows, : 2 * width] = even[:, cols]
                values[rows, 2 * width :] = odd[:, cols]
        placed = dot_nn(values[...], place).astype(BF)
        for parity in range(2):
            for pair in range(2):
                rows = slice((2 * parity + pair) * chans, (2 * parity + pair + 1) * chans)
                first = 8 * step + 4 * pair + parity
                out_ref[first] = placed[rows, : 2 * width]
                out_ref[first + 2] = placed[rows, 2 * width :]


def image_gradient(place, flips, grads, parts, halo, width):
    pixels, span = grads[0].shape
    outs, part_span = parts[0].shape
    full = span * len(grads)
    chans = outs // 9
    kernel = functools.partial(image_kernel, len(grads), len(parts), flips, width)
    anywhere = pl.BlockSpec(memory_space=pltpu.HBM)
    return pl.pallas_call(
        kernel,
        out_shape=jax.ShapeDtypeStruct((2 * pixels // width, chans, 2 * width), BF),
        in_specs=[pl.BlockSpec(memory_space=pltpu.SMEM), pl.BlockSpec(memory_space=pltpu.VMEM)]
        + [anywhere] * (len(grads) + len(parts)),
        out_specs=pl.BlockSpec(memory_space=pltpu.VMEM),
        scratch_shapes=[
            pltpu.VMEM((pixels, full), BF),
            pltpu.VMEM((outs, full), BF),
            pltpu.VMEM((4 * chans, 4 * width), BF),
            pltpu.SemaphoreType.DMA((len(grads), pixels // (4 * width))),
            pltpu.SemaphoreType.DMA((len(parts),)),
        ],
        compiler_params=params(32),
        cost_estimate=SMALL,
        name="image_grad",
    )(place, halo, *grads, *parts)


def edge_kernel(grad_count, part_count, flips, width, place_ref, *refs):
    grads, parts = refs[:grad_count], refs[grad_count : grad_count + part_count]
    out_ref, grad_all, part_all, grad_sem, part_sem = refs[grad_count + part_count :]
    span = grads[0].shape[1]
    outs, part_span = parts[0].shape
    chans = outs // 9
    tops = 3 * chans
    copies = []
    for index in range(part_count):
        start = pl.multiple_of(part_place(place_ref, flips, index) * part_span, part_span)
        copies.append(
            pltpu.make_async_copy(
                parts[index].at[pl.ds(0, tops)], part_all.at[:, pl.ds(start, part_span)], part_sem.at[index]
            )
        )
    for index in range(grad_count):
        start = pl.multiple_of(grad_place(place_ref, flips, index) * span, span)
        copies.append(
            pltpu.make_async_copy(
                grads[index].at[pl.ds(0, 2 * width)], grad_all.at[:, pl.ds(start, span)], grad_sem.at[index]
            )
        )
    for copy in copies:
        copy.start()
    for copy in copies:
        copy.wait()
    terms = dot_nt(part_all[...], grad_all[...])
    lane = iota((chans, 2 * width), 1)
    moved = jnp.where(lane % width == width - 1, 0.0, pltpu.roll(terms[:chans], 2 * width - 1, 1))
    even, odd = terms[chans : 2 * chans], terms[2 * chans :] + moved
    out_ref[:chans] = pltpu.roll(even, width, 1)
    out_ref[chans:] = pltpu.roll(odd, width, 1)


def edge_terms(place, flips, grads, parts, width):
    span = grads[0].shape[1]
    outs, part_span = parts[0].shape
    full = span * len(grads)
    kernel = functools.partial(edge_kernel, len(grads), len(parts), flips, width)
    anywhere = pl.BlockSpec(memory_space=pltpu.HBM)
    return pl.pallas_call(
        kernel,
        out_shape=jax.ShapeDtypeStruct((2 * outs // 9, 2 * width), F32),
        in_specs=[pl.BlockSpec(memory_space=pltpu.SMEM)] + [anywhere] * (len(grads) + len(parts)),
        out_specs=pl.BlockSpec(memory_space=pltpu.VMEM),
        scratch_shapes=[
            pltpu.VMEM((2 * width, full), BF),
            pltpu.VMEM((outs // 3, full), BF),
            pltpu.SemaphoreType.DMA((len(grads),)),
            pltpu.SemaphoreType.DMA((len(parts),)),
        ],
        compiler_params=params(16),
        cost_estimate=SMALL,
        name="edge",
    )(place, *grads, *parts)


CUTS = 3


def partial_kernel(count, chosen_blocks, place_ref, taps_ref, *refs):
    picks = len(chosen_blocks)
    core, turn = place_ref[0] & 1, (place_ref[1] >> 1) & 1
    blocks, outs = refs[:count], refs[count : count + picks]
    taps, grads, sums, grad_sems, taps_sems, out_sems = refs[count + picks :]
    rows = taps.shape[1]
    part = lambda ref, cut: ref.at[pl.ds(cut * rows, rows)]

    def chosen(pick, index):
        return pltpu.make_async_copy(blocks[index], grads.at[pick], grad_sems.at[pick])

    def out_copy(pick, cut):
        return pltpu.make_async_copy(sums.at[pick, cut], part(outs[pick], cut), out_sems.at[pick, cut])

    taps_in = [pltpu.make_async_copy(part(taps_ref, cut), taps.at[cut], taps_sems.at[cut]) for cut in range(CUTS)]

    def start(pick):
        kept, phase, base = chosen_blocks[pick]
        step = base + ((2 * phase + (core if kept else 1 - core) + turn) & 3)
        for index in range(count):

            @pl.when(step == index)
            def _():
                chosen(pick, index).start()

    start(0)
    for copy in taps_in:
        copy.start()
    for pick in range(1, picks):
        start(pick)
    for pick in range(picks):
        chosen(pick, 0).wait()
        for cut in range(CUTS):
            if pick == 0:
                taps_in[cut].wait()
            sums[pick, cut] = dot_nn(taps[cut], grads[pick]).astype(BF)
            out_copy(pick, cut).start()
    for pick in range(picks):
        for cut in range(CUTS):
            out_copy(pick, cut).wait()


def kernel_partials(place, taps, blocks, chosen):
    outs, pixels = taps.shape
    span = blocks[0].shape[1]
    rows = outs // CUTS
    picks = len(chosen)
    anywhere = pl.BlockSpec(memory_space=pltpu.HBM)
    return pl.pallas_call(
        functools.partial(partial_kernel, len(blocks), tuple(chosen)),
        out_shape=(jax.ShapeDtypeStruct((outs, span), BF),) * picks,
        in_specs=[pl.BlockSpec(memory_space=pltpu.SMEM)] + [anywhere] * (1 + len(blocks)),
        out_specs=(anywhere,) * picks,
        scratch_shapes=[
            pltpu.VMEM((CUTS, rows, pixels), BF),
            pltpu.VMEM((picks, pixels, span), BF),
            pltpu.VMEM((picks, CUTS, rows, span), BF),
            pltpu.SemaphoreType.DMA((picks,)),
            pltpu.SemaphoreType.DMA((CUTS,)),
            pltpu.SemaphoreType.DMA((picks, CUTS)),
        ],
        compiler_params=params(16),
        cost_estimate=SMALL,
        name="partials",
    )(place, taps, *blocks)


def step_along(value, axis, steps):
    count = lax.axis_size(axis)
    return lax.ppermute(
        value, axis, [(source, source + steps) for source in range(count) if 0 <= source + steps < count]
    )


def swap(value, axis, bits):
    return lax.ppermute(value, axis, [(source, source ^ bits) for source in range(lax.axis_size(axis))])


def kernel_sum_plain(taps, grads):
    partial = jnp.concatenate([dot_nn(taps, grad).astype(BF) for grad in grads], axis=1)
    return lax.psum_scatter(partial, "pix", scatter_dimension=1, tiled=True).astype(F32)


def kept_step(core, outer, phase):
    return (2 * phase + core + outer % 2) % 4


def kept_here(pix, outer, phase):
    return (outer - kept_step(pix % 2, outer, phase)) % 4 // 2 == pix // 2


def send_over(value, phase):
    pairs = []
    for pix in range(4):
        for ch in range(8):
            if not kept_here(pix, ch // 2, phase):
                pairs.append((pix * 8 + ch, (pix ^ 2) * 8 + ch))
    return lax.ppermute(value, ("pix", "ch"), pairs)


def ring(value):
    return lax.ppermute(value, "ch", [(source, (source + 2) % 8) for source in range(8)])


def shards(image_in, pre_act, grad_out, conv_weight, mix_weight):
    tile_rows, width, chans = grad_out.shape
    in_chans = image_in.shape[1]
    pix_count, ch_count = lax.axis_size("pix"), lax.axis_size("ch")
    pix, ch = lax.axis_index("pix"), lax.axis_index("ch")
    first_tile = pix % TILES == 0
    last_tile = pix % TILES == TILES - 1
    pixels = tile_rows * width
    scale = 1.0 / float(pix_count * pixels) ** 0.5

    tie = lax.optimization_barrier
    place = jnp.stack([pix, ch]).astype(jnp.int32)
    prev_row = step_along(image_in[-1], "pix", 1)
    grad_pre, mix_part = pre_gradient(
        grad_out.reshape(pixels, chans),
        pre_act.reshape(pixels, chans),
        mix_weight.reshape(chans, GROUP_WIDTH),
    )
    kernel_own = conv_weight.reshape(9 * in_chans, -1)
    rings = pix_count == 4 and ch_count == 8
    if rings:
        mix_other = swap(mix_part, "pix", 2)
        kernel_own, prev_row, mix_other = tie((kernel_own, prev_row, mix_other))
    taps = image_taps(image_in, jnp.where(first_tile, jnp.zeros_like(prev_row), prev_row))

    if rings:
        kernel_x = swap(kernel_own, "pix", 2)
        kernel_core = swap(kernel_own, "pix", 1)
        mix_sum = mix_part + mix_other
        mix_sum = mix_sum + swap(mix_sum, "pix", 1)
        near, far = [grad_pre], [swap(grad_pre, "ch", 1)]
        totals, arrived = [[None] * 2, [None] * 2], [[None] * 2, [None] * 2]

        def add_up(sums, phase, half):
            total = sums[1] + swap(sums[0], "pix", 1)
            totals[phase][half] = total
            arrived[phase][half] = send_over(total, phase)

        near.append(ring(near[0]))
        near[1], far[0], taps, mix_sum = tie((near[1], far[0], taps, mix_sum))
        far.append(swap(near[1], "ch", 1))
        near.append(ring(near[1]))
        near[2], far[1], kernel_core = tie((near[2], far[1], kernel_core))
        far.append(swap(near[2], "ch", 1))
        near.append(ring(near[2]))
        first = kernel_partials(place, taps, near[:3], [(0, 0, 0), (1, 0, 0)])
        near[3], far[2], first = tie((near[3], far[2], first))
        far.append(swap(near[3], "ch", 1))
        add_up(first, 0, 0)
        kernel_xcore = swap(kernel_x, "pix", 1)
        second = kernel_partials(
            place, taps, near + far[:3], [(0, 0, 4), (0, 1, 0), (1, 0, 4), (1, 1, 0)]
        )
        far[3], arrived[0][0], second, kernel_xcore = tie((far[3], arrived[0][0], second, kernel_xcore))
        add_up(second[::2], 0, 1)
        add_up(second[1::2], 1, 0)
        third = kernel_partials(place, taps, far, [(0, 1, 0), (1, 1, 0)])
        third, _ = tie((third, (totals[0][1], totals[1][0])))
        add_up(third, 1, 1)
        core, outer, side = pix % 2, ch // 2, ch % 2
        mine = kept_here(pix, outer, 0)
        halves = [
            jnp.where(mine, totals[0][half], totals[1][half]).astype(F32)
            + jnp.where(mine, arrived[0][half], arrived[1][half]).astype(F32)
            for half in range(2)
        ]
        grad_conv = jnp.concatenate(
            [jnp.where(side == 0, halves[0], halves[1]), jnp.where(side == 0, halves[1], halves[0])], axis=1
        )
        grads = near + far
        parts = [kernel_own, kernel_core, kernel_x, kernel_xcore]
        edge_at, _ = tie((place, third))
        image_at = (place, totals[1][1])
    else:
        mix_sum = lax.psum(mix_part, "pix")
        grad_all = lax.all_gather(grad_pre, "ch", axis=0)
        kernel_all = lax.all_gather(kernel_own, "pix", axis=0)
        grads = [grad_all[index] for index in range(ch_count)]
        parts = [kernel_all[index] for index in range(pix_count)]
        grad_conv = kernel_sum_plain(taps, grads)
        edge_at, image_at = place, (place,)
    edge = step_along(edge_terms(edge_at, rings, grads, parts, width), "pix", -1)
    edge = jnp.where(last_tile, jnp.zeros_like(edge), edge)
    image_at = tie(image_at)[0]
    grad_in = image_gradient(image_at, rings, grads, parts, edge, width)
    grad_mix = (mix_sum * scale).reshape(mix_weight.shape)
    return (grad_in, (grad_conv * scale).reshape(conv_weight.shape), grad_mix)


def solution(mesh):
    in_specs = (
        P("pix", "ch", None),
        P("pix", None, "ch"),
        P("pix", None, "ch"),
        P(None, None, "ch", "pix"),
        P("ch", None, None),
    )
    out_specs = (P("pix", "ch", None), P(None, None, "ch", "pix"), P("ch", None, None))
    return jax.shard_map(shards, mesh=mesh, in_specs=in_specs, out_specs=out_specs, check_vma=False)
```

```python
import functools

import jax
import jax.numpy as jnp
from jax import lax
from jax.experimental import pallas as pl
from jax.experimental.pallas import tpu as pltpu
from jax.sharding import PartitionSpec as P

TILES = 4
CUTS = 3
GROUP_WIDTH = 64
BF = jnp.bfloat16
F32 = jnp.float32
SMALL = pl.CostEstimate(flops=1, bytes_accessed=1, transcendentals=0)


def params(mebibytes):
    return pltpu.CompilerParams(vmem_limit_bytes=mebibytes * 2**20)


def dot_nn(a, b):
    return lax.dot_general(a, b, (((1,), (0,)), ((), ())), preferred_element_type=F32)


def dot_nt(a, b):
    return lax.dot_general(a, b, (((1,), (1,)), ((), ())), preferred_element_type=F32)


def dot_tn(a, b):
    return lax.dot_general(a, b, (((0,), (0,)), ((), ())), preferred_element_type=F32)


def iota(shape, dim):
    return lax.broadcasted_iota(jnp.int32, shape, dim)


def pre_kernel(grad_ref, pre_ref, mix_ref, out_ref, mix_out_ref):
    chans = grad_ref.shape[1]
    spread = (iota((GROUP_WIDTH, chans), 0) == iota((GROUP_WIDTH, chans), 1) % GROUP_WIDTH).astype(BF)
    same = iota((chans, chans), 0) // GROUP_WIDTH == iota((chans, chans), 1) // GROUP_WIDTH
    blocks = jnp.where(same, dot_nn(mix_ref[...], spread), 0.0).astype(BF)
    grad = grad_ref[...]
    pre = pre_ref[...].astype(F32)
    sig = jax.nn.sigmoid(pre)
    act = (pre * sig).astype(BF)
    grad_act = dot_nt(grad, blocks)
    out_ref[...] = (grad_act * (sig * (1.0 + pre * (1.0 - sig)))).astype(BF)
    full = jnp.where(same, dot_tn(act, grad), 0.0)
    total = full
    for step in range(1, chans // GROUP_WIDTH):
        total = total + pltpu.roll(full, step * GROUP_WIDTH, 1)
    mix_out_ref[...] = total[:, :GROUP_WIDTH]


def pre_gradient(grad_out, pre_act, mix_weight):
    pixels, chans = grad_out.shape
    return pl.pallas_call(
        pre_kernel,
        out_shape=(
            jax.ShapeDtypeStruct((pixels, chans), BF),
            jax.ShapeDtypeStruct((chans, GROUP_WIDTH), F32),
        ),
        compiler_params=params(60),
        cost_estimate=SMALL,
        name="pre_grad",
    )(grad_out, pre_act, mix_weight)


def taps_kernel(image_ref, prev_ref, out_ref):
    rows, chans, width = image_ref.shape
    half = width // 2
    col_in = iota((2 * width, 6 * half), 0)
    col_out = iota((2 * width, 6 * half), 1)
    pick = (
        (col_in // width == (col_out % width) // half)
        & (col_in % width == 2 * (col_out % half) + col_out // width - 1)
    ).astype(BF)
    for pair in range(rows // 4):
        for row_tap in range(3):
            first = 4 * pair + row_tap - 1
            upper = prev_ref[...] if first < 0 else image_ref[first]
            both = jnp.concatenate([upper, image_ref[first + 2]], axis=1)
            picked = dot_nn(both, pick).astype(BF)
            for col_tap in range(3):
                tap = 3 * row_tap + col_tap
                out_ref[tap * chans : (tap + 1) * chans, pair * width : (pair + 1) * width] = picked[
                    :, col_tap * width : (col_tap + 1) * width
                ]


def image_taps(image_in, prev_row):
    rows, chans, width = image_in.shape
    pixels = rows * width // 4
    return pl.pallas_call(
        taps_kernel,
        out_shape=jax.ShapeDtypeStruct((9 * chans, pixels), BF),
        compiler_params=params(60),
        cost_estimate=SMALL,
        name="taps",
    )(image_in, prev_row)


def grad_place(place_ref, flips, index):
    if not flips:
        return index
    return ((place_ref[1] + 8 - 2 * (index % 4)) & 7) ^ (index // 4)


def part_place(place_ref, flips, index):
    return place_ref[0] ^ index if flips else index


def interleave(width):
    place_in = iota((4 * width, 4 * width), 0)
    place_out = iota((4 * width, 4 * width), 1)
    return (
        ((place_in % (2 * width)) // width == place_out // (2 * width))
        & (2 * (place_in % width) + place_in // (2 * width) == place_out % (2 * width))
    ).astype(BF)


def image_kernel(
    grad_count, part_count, flips, width, place_ref, *refs
):
    grads, parts = refs[:grad_count], refs[grad_count : grad_count + part_count]
    out_ref, last_ref, edge_ref, grad_all, part_all, values, grad_sem, part_sem = refs[grad_count + part_count :]
    pixels, span = grads[0].shape
    outs, part_span = parts[0].shape
    chans = outs // 9
    pairs = pixels // (2 * width)
    tile = pixels

    def part_copy(index):
        start = pl.multiple_of(part_place(place_ref, flips, index) * part_span, part_span)
        return pltpu.make_async_copy(parts[index], part_all.at[:, pl.ds(start, part_span)], part_sem.at[index])

    def grad_copy(index):
        rows = grads[index].shape[0]
        start = pl.multiple_of(grad_place(place_ref, flips, min(index, grad_count - 2) if flips else index) * span, span)
        first = rows if flips and index == grad_count - 1 else 0
        return pltpu.make_async_copy(
            grads[index], grad_all.at[pl.ds(first, rows), pl.ds(start, span)], grad_sem.at[index]
        )

    for index in range(part_count):
        part_copy(index).start()
    for index in range(grad_count):
        grad_copy(index).start()

    lane = iota((chans, tile), 1)
    last_col = lane % width == width - 1
    row_end = lane >= tile - width
    place = interleave(width)

    def left(value):
        return jnp.where(last_col, 0.0, pltpu.roll(value, tile - 1, 1))

    def up_terms(terms):
        even, odd = terms[chans : 2 * chans], terms[2 * chans : 3 * chans] + left(terms[:chans])
        return pltpu.roll(even, tile - width, 1), pltpu.roll(odd, tile - width, 1)

    def tap_row(tap):
        return dot_nt(part_all[3 * tap * chans : 3 * (tap + 1) * chans], grad_all[...])

    third = lambda terms, index: terms[index * chans : (index + 1) * chans]
    for index in range(part_count):
        part_copy(index).wait()
    for index in range(grad_count):
        grad_copy(index).wait()
    upper = tap_row(0)
    own = up_terms(upper)
    middle = tap_row(1)
    lower = tap_row(2)
    phases = (
        (third(middle, 1), third(middle, 2) + left(third(middle, 0))),
        (
            third(lower, 1) + jnp.where(row_end, 0.0, own[0]),
            third(lower, 2) + left(third(lower, 0)) + jnp.where(row_end, 0.0, own[1]),
        ),
    )
    for index in range(2):
        at = slice(index * chans, (index + 1) * chans)
        edge_ref[at] = own[index][:, tile - 2 * width :]
        last_ref[at] = phases[1][index][:, tile - 2 * width :]
    for parity in range(2):
        even, odd = (value.astype(BF) for value in phases[parity])
        for pair in range(pairs):
            cols = slice(pair * 2 * width, (pair + 1) * 2 * width)
            at = slice((pairs * parity + pair) * chans, (pairs * parity + pair + 1) * chans)
            values[at, : 2 * width] = even[:, cols]
            values[at, 2 * width :] = odd[:, cols]
    placed = dot_nn(values[...], place).astype(BF)
    for parity in range(2):
        for pair in range(pairs):
            at = slice((pairs * parity + pair) * chans, (pairs * parity + pair + 1) * chans)
            first = 4 * pair + parity
            out_ref[first] = placed[at, : 2 * width]
            out_ref[first + 2] = placed[at, 2 * width :]


def image_gradient(place, flips, grads, parts, width):
    pixels, span = grads[0].shape
    outs, part_span = parts[0].shape
    full = part_span * len(parts)
    if flips:
        grads = [*grads[:-1], *grads[-1]]
    chans = outs // 9
    kernel = functools.partial(image_kernel, len(grads), len(parts), flips, width)
    anywhere = pl.BlockSpec(memory_space=pl.ANY)
    return pl.pallas_call(
        kernel,
        out_shape=(
            jax.ShapeDtypeStruct((2 * pixels // width, chans, 2 * width), BF),
            jax.ShapeDtypeStruct((2 * chans, 2 * width), F32),
            jax.ShapeDtypeStruct((2 * chans, 2 * width), F32),
        ),
        in_specs=[pl.BlockSpec(memory_space=pltpu.SMEM)] + [anywhere] * (len(grads) + len(parts)),
        out_specs=(pl.BlockSpec(memory_space=pltpu.VMEM),) * 3,
        scratch_shapes=[
            pltpu.VMEM((pixels, full), BF),
            pltpu.VMEM((outs, full), BF),
            pltpu.VMEM((pixels // width * chans, 4 * width), BF),
            pltpu.SemaphoreType.DMA((len(grads),)),
            pltpu.SemaphoreType.DMA((len(parts),)),
        ],
        compiler_params=params(60),
        cost_estimate=SMALL,
        name="image_grad",
    )(place, *grads, *parts)


def last_row(image_ref, last_ref, edge_ref, out_ref, row, sem, place_ref):
    doubled, width = last_ref.shape
    chans, half = doubled // 2, width // 2
    inside = place_ref[0] % TILES != TILES - 1
    total = last_ref[...] + jnp.where((iota((doubled, width), 1) >= half) & inside, edge_ref[...], 0.0)
    both = jnp.concatenate([total[:chans], total[chans:]], axis=1).astype(BF)
    row[...] = dot_nn(both, interleave(half))[:, width:].astype(BF)
    copy = pltpu.make_async_copy(row, out_ref.at[out_ref.shape[0] - 1], sem)
    copy.start()
    return copy


def finish_kernel(place_ref, image_ref, last_ref, edge_ref, out_ref, row, sem):
    last_row(image_ref, last_ref, edge_ref, out_ref, row, sem, place_ref).wait()


def finish_both_kernel(scale, place_ref, image_ref, last_ref, edge_ref, *refs):
    totals, others, (out_ref, conv_ref) = refs[:4], refs[4:7], refs[7:9]
    row, sem, held, sums, in_sems, out_sems = refs[9:]
    outs, span = totals[0].shape
    rows = outs // CUTS
    core, outer, side = place_ref[0] & 1, place_ref[1] >> 1, place_ref[1] & 1
    step = (core + (outer & 1)) & 3
    mine = (((outer - step) & 3) >> 1) == (place_ref[0] >> 1)
    pairs = ((totals[0], others[0], totals[1], others[1]), (totals[2], others[1], totals[3], others[2]))

    def load(ref, half, which, cut):
        return pltpu.make_async_copy(
            ref.at[pl.ds(cut * rows, rows)], held.at[half, which, cut], in_sems.at[half, which, cut]
        )

    def store(half, cut):
        start = pl.multiple_of((side if half == 0 else 1 - side) * span, span)
        return pltpu.make_async_copy(
            sums.at[half, cut], conv_ref.at[pl.ds(cut * rows, rows), pl.ds(start, span)], out_sems.at[half, cut]
        )

    for cut in range(CUTS):
        for half in range(2):
            for which in range(2):

                @pl.when(mine)
                def _():
                    load(pairs[half][which], half, which, cut).start()

                @pl.when(jnp.logical_not(mine))
                def _():
                    load(pairs[half][2 + which], half, which, cut).start()

    row_copy = last_row(image_ref, last_ref, edge_ref, out_ref, row, sem, place_ref)
    for cut in range(CUTS):
        for half in range(2):
            for which in range(2):
                load(totals[0], half, which, cut).wait()
            sums[half, cut] = (held[half, 0, cut].astype(F32) + held[half, 1, cut].astype(F32)) * scale
            store(half, cut).start()
    for cut in range(CUTS):
        for half in range(2):
            store(half, cut).wait()
    row_copy.wait()


def finish_image(place, image, last, edge):
    anywhere, here = pl.BlockSpec(memory_space=pl.ANY), pl.BlockSpec(memory_space=pltpu.VMEM)
    return pl.pallas_call(
        finish_kernel,
        out_shape=jax.ShapeDtypeStruct(image.shape, BF),
        in_specs=[pl.BlockSpec(memory_space=pltpu.SMEM), anywhere, here, here],
        out_specs=anywhere,
        scratch_shapes=[pltpu.VMEM(image.shape[1:], BF), pltpu.SemaphoreType.DMA(())],
        input_output_aliases={1: 0},
        compiler_params=params(60),
        cost_estimate=SMALL,
        name="finish",
    )(place, image, last, edge)


def finish_both(place, image, last, edge, totals, others, scale):
    anywhere, here = pl.BlockSpec(memory_space=pl.ANY), pl.BlockSpec(memory_space=pltpu.VMEM)
    outs, span = totals[0].shape
    rows = outs // CUTS
    return pl.pallas_call(
        functools.partial(finish_both_kernel, scale),
        out_shape=(jax.ShapeDtypeStruct(image.shape, BF), jax.ShapeDtypeStruct((outs, 2 * span), F32)),
        in_specs=[pl.BlockSpec(memory_space=pltpu.SMEM), anywhere, here, here] + [anywhere] * 7,
        out_specs=(anywhere, anywhere),
        scratch_shapes=[
            pltpu.VMEM(image.shape[1:], BF),
            pltpu.SemaphoreType.DMA(()),
            pltpu.VMEM((2, 2, CUTS, rows, span), BF),
            pltpu.VMEM((2, CUTS, rows, span), F32),
            pltpu.SemaphoreType.DMA((2, 2, CUTS)),
            pltpu.SemaphoreType.DMA((2, CUTS)),
        ],
        input_output_aliases={1: 0},
        compiler_params=params(60),
        cost_estimate=SMALL,
        name="finish",
    )(place, image, last, edge, *totals, *others)


def partial_kernel(count, split, chosen_blocks, place_ref, taps_ref, *refs):
    picks = len(chosen_blocks)
    core, turn = place_ref[0] & 1, (place_ref[1] >> 1) & 1
    whole = count - 1 if split else count
    inputs = whole + (2 if split else 0)
    blocks, outs = refs[:inputs], refs[inputs : inputs + picks]
    taps, grads, sums, grad_sems, taps_sems, out_sems = refs[inputs + picks :]
    half = taps_ref.shape[1] // 2
    rows = taps.shape[1]
    part = lambda ref, cut: ref.at[pl.ds(cut * rows, rows)]

    def chosen(pick, index):
        return pltpu.make_async_copy(blocks[index], grads.at[pick], grad_sems.at[pick])

    def out_copy(pick, cut):
        return pltpu.make_async_copy(sums.at[pick, cut], part(outs[pick], cut), out_sems.at[pick, cut])

    taps_in = [pltpu.make_async_copy(part(taps_ref, cut), taps.at[cut], taps_sems.at[cut]) for cut in range(CUTS)]

    def start(pick):
        kept, phase, base = chosen_blocks[pick]
        step = base + ((2 * phase + (core if kept else 1 - core) + turn) & 3)
        for index in range(count):

            @pl.when(step == index)
            def _():
                if index < whole:
                    chosen(pick, index).start()
                else:
                    for piece in range(2):
                        pltpu.make_async_copy(
                            blocks[whole + piece],
                            grads.at[pick, pl.ds(piece * half, half)],
                            grad_sems.at[pick],
                        ).start()

    start(0)
    for copy in taps_in:
        copy.start()
    for pick in range(1, picks):
        start(pick)
    for pick in range(picks):
        chosen(pick, 0).wait()
        for cut in range(CUTS):
            if pick == 0:
                taps_in[cut].wait()
            sums[pick, cut] = dot_nn(taps[cut], grads[pick]).astype(BF)
            out_copy(pick, cut).start()
    for pick in range(picks):
        for cut in range(CUTS):
            out_copy(pick, cut).wait()


def kernel_partials(place, taps, blocks, chosen):
    outs, pixels = taps.shape
    span = blocks[0].shape[1]
    count, split = len(blocks), isinstance(blocks[-1], tuple)
    if split:
        blocks = [*blocks[:-1], *blocks[-1]]
    rows = outs // CUTS
    picks = len(chosen)
    anywhere = pl.BlockSpec(memory_space=pl.ANY)
    return pl.pallas_call(
        functools.partial(partial_kernel, count, split, tuple(chosen)),
        out_shape=(jax.ShapeDtypeStruct((outs, span), BF),) * picks,
        in_specs=[pl.BlockSpec(memory_space=pltpu.SMEM)] + [anywhere] * (1 + len(blocks)),
        out_specs=(anywhere,) * picks,
        scratch_shapes=[
            pltpu.VMEM((CUTS, rows, pixels), BF),
            pltpu.VMEM((picks, pixels, span), BF),
            pltpu.VMEM((picks, CUTS, rows, span), BF),
            pltpu.SemaphoreType.DMA((picks,)),
            pltpu.SemaphoreType.DMA((CUTS,)),
            pltpu.SemaphoreType.DMA((picks, CUTS)),
        ],
        compiler_params=params(60),
        cost_estimate=SMALL,
        name="partials",
    )(place, taps, *blocks)


def step_along(value, axis, steps):
    count = lax.axis_size(axis)
    return lax.ppermute(
        value, axis, [(source, source + steps) for source in range(count) if 0 <= source + steps < count]
    )


def swap(value, axis, bits):
    return lax.ppermute(value, axis, [(source, source ^ bits) for source in range(lax.axis_size(axis))])


def kernel_sum_plain(taps, grads):
    partial = jnp.concatenate([dot_nn(taps, grad).astype(BF) for grad in grads], axis=1)
    return lax.psum_scatter(partial, "pix", scatter_dimension=1, tiled=True).astype(F32)


def kept_step(core, outer, phase):
    return (2 * phase + core + outer % 2) % 4


def kept_here(pix, outer, phase):
    return (outer - kept_step(pix % 2, outer, phase)) % 4 // 2 == pix // 2


def send_over(value, phase):
    pairs = []
    for pix in range(4):
        for ch in range(8):
            if not kept_here(pix, ch // 2, phase):
                pairs.append((pix * 8 + ch, (pix ^ 2) * 8 + ch))
    return lax.ppermute(value, ("pix", "ch"), pairs)


def ring(value):
    return lax.ppermute(value, "ch", [(source, (source + 2) % 8) for source in range(8)])


def shards(image_in, pre_act, grad_out, conv_weight, mix_weight):
    tile_rows, width, chans = grad_out.shape
    in_chans = image_in.shape[1]
    pix_count, ch_count = lax.axis_size("pix"), lax.axis_size("ch")
    pix, ch = lax.axis_index("pix"), lax.axis_index("ch")
    first_tile = pix % TILES == 0
    last_tile = pix % TILES == TILES - 1
    pixels = tile_rows * width
    scale = 1.0 / float(pix_count * pixels) ** 0.5

    tie = lax.optimization_barrier
    place = jnp.stack([pix, ch]).astype(jnp.int32)
    prev_row = step_along(image_in[-1], "pix", 1)
    grad_pre, mix_part = pre_gradient(
        grad_out.reshape(pixels, chans),
        pre_act.reshape(pixels, chans),
        mix_weight.reshape(chans, GROUP_WIDTH),
    )
    kernel_own = conv_weight.reshape(9 * in_chans, -1)
    rings = pix_count == 4 and ch_count == 8
    taps = image_taps(image_in, jnp.where(first_tile, jnp.zeros_like(prev_row), prev_row))

    if rings:
        near, far = [grad_pre], [swap(grad_pre, "ch", 1)]
        near.append(ring(near[0]))
        mix_sum = mix_part + swap(mix_part, "pix", 2)
        grad_mix = (mix_sum + swap(mix_sum, "pix", 1)) * scale
        totals = [[None] * 2, [None] * 2]

        def add_up(sums, phase, half):
            totals[phase][half] = sums[1] + swap(sums[0], "pix", 1)

        near[1], far[0], taps, grad_mix, kernel_own = tie((near[1], far[0], taps, grad_mix, kernel_own))
        far.append(swap(near[1], "ch", 1))
        near.append(ring(near[1]))
        kernel_x = swap(kernel_own, "pix", 2)
        kernel_core = swap(kernel_own, "pix", 1)
        near[2], far[1], kernel_core = tie((near[2], far[1], kernel_core))
        far.append(swap(near[2], "ch", 1))
        near.append(ring(near[2]))
        first = kernel_partials(place, taps, near[:3], [(0, 0, 0), (1, 0, 0)])
        near[3], far[2], first, kernel_x = tie((near[3], far[2], first, kernel_x))
        half = pixels // 2
        far.append((swap(near[3][:half], "ch", 1), ring(far[2][half:])))
        add_up(first, 0, 0)
        kernel_xcore = swap(kernel_x, "pix", 1)
        second = kernel_partials(
            place, taps, near + far[:3], [(0, 0, 4), (0, 1, 0), (1, 0, 4), (1, 1, 0)]
        )
        far[3], totals[0][0], second, kernel_xcore = tie((far[3], totals[0][0], second, kernel_xcore))
        mine = kept_here(pix, ch // 2, 0)
        arrived_first = send_over(totals[0][0], 0)
        add_up(second[::2], 0, 1)
        add_up(second[1::2], 1, 0)
        crossing = jnp.where(mine, totals[1][0], totals[0][1])
        crossing, taps = tie((crossing, taps))
        arrived_both = swap(crossing, "pix", 2)
        third = kernel_partials(place, taps, far, [(0, 1, 0), (1, 1, 0)])
        third, arrived_first = tie((third, arrived_first))
        add_up(third, 1, 1)
        arrived_last = send_over(totals[1][1], 1)
        grads = near + far
        parts = [kernel_own, kernel_core, kernel_x, kernel_xcore]
        image_at = (place, totals[1][1])
    else:
        grad_mix = lax.psum(mix_part, "pix") * scale
        grad_all = lax.all_gather(grad_pre, "ch", axis=0)
        kernel_all = lax.all_gather(kernel_own, "pix", axis=0)
        grads = [grad_all[index] for index in range(ch_count)]
        parts = [kernel_all[index] for index in range(pix_count)]
        grad_conv = kernel_sum_plain(taps, grads)
        image_at = (place,)
    grad_in, last, edge = image_gradient(tie(image_at)[0], rings, grads, parts, width)
    edge = step_along(edge, "pix", -1)
    if rings:
        grad_in, grad_conv = finish_both(
            place,
            grad_in,
            last,
            edge,
            [totals[0][0], totals[1][0], totals[0][1], totals[1][1]],
            [arrived_first, arrived_both, arrived_last],
            scale,
        )
    else:
        grad_in = finish_image(place, grad_in, last, edge)
        grad_conv = grad_conv * scale
    return (grad_in, grad_conv.reshape(conv_weight.shape), grad_mix.reshape(mix_weight.shape))


def solution(mesh):
    in_specs = (
        P("pix", "ch", None),
        P("pix", None, "ch"),
        P("pix", None, "ch"),
        P(None, None, "ch", "pix"),
        P("ch", None, None),
    )
    out_specs = (P("pix", "ch", None), P(None, None, "ch", "pix"), P("ch", None, None))
    return jax.shard_map(shards, mesh=mesh, in_specs=in_specs, out_specs=out_specs, check_vma=False)
```

```python
import functools

import jax
import jax.numpy as jnp
from jax import lax
from jax.experimental import pallas as pl
from jax.experimental.pallas import tpu as pltpu
from jax.sharding import PartitionSpec as P

TILES = 4
CUTS = 3
GROUP_WIDTH = 64
BF = jnp.bfloat16
F32 = jnp.float32
SMALL = pl.CostEstimate(flops=1, bytes_accessed=1, transcendentals=0)


def params(mebibytes):
    return pltpu.CompilerParams(vmem_limit_bytes=mebibytes * 2**20)


def dot_nn(a, b):
    return lax.dot_general(a, b, (((1,), (0,)), ((), ())), preferred_element_type=F32)


def dot_nt(a, b):
    return lax.dot_general(a, b, (((1,), (1,)), ((), ())), preferred_element_type=F32)


def dot_tn(a, b):
    return lax.dot_general(a, b, (((0,), (0,)), ((), ())), preferred_element_type=F32)


def iota(shape, dim):
    return lax.broadcasted_iota(jnp.int32, shape, dim)


def pre_kernel(grad_ref, pre_ref, mix_ref, out_ref, mix_out_ref):
    chans = grad_ref.shape[1]
    spread = (iota((GROUP_WIDTH, chans), 0) == iota((GROUP_WIDTH, chans), 1) % GROUP_WIDTH).astype(BF)
    same = iota((chans, chans), 0) // GROUP_WIDTH == iota((chans, chans), 1) // GROUP_WIDTH
    blocks = jnp.where(same, dot_nn(mix_ref[...], spread), 0.0).astype(BF)
    grad = grad_ref[...]
    pre = pre_ref[...].astype(F32)
    sig = jax.nn.sigmoid(pre)
    act = (pre * sig).astype(BF)
    grad_act = dot_nt(grad, blocks)
    out_ref[...] = (grad_act * (sig * (1.0 + pre * (1.0 - sig)))).astype(BF)
    full = jnp.where(same, dot_tn(act, grad), 0.0)
    total = full
    for step in range(1, chans // GROUP_WIDTH):
        total = total + pltpu.roll(full, step * GROUP_WIDTH, 1)
    mix_out_ref[...] = total[:, :GROUP_WIDTH]


def pre_gradient(grad_out, pre_act, mix_weight):
    pixels, chans = grad_out.shape
    return pl.pallas_call(
        pre_kernel,
        out_shape=(
            jax.ShapeDtypeStruct((pixels, chans), BF),
            jax.ShapeDtypeStruct((chans, GROUP_WIDTH), F32),
        ),
        compiler_params=params(60),
        cost_estimate=SMALL,
        name="pre_grad",
    )(grad_out, pre_act, mix_weight)


def taps_kernel(image_ref, prev_ref, out_ref):
    rows, chans, width = image_ref.shape
    half = width // 2
    col_in = iota((2 * width, 6 * half), 0)
    col_out = iota((2 * width, 6 * half), 1)
    pick = (
        (col_in // width == (col_out % width) // half)
        & (col_in % width == 2 * (col_out % half) + col_out // width - 1)
    ).astype(BF)
    for pair in range(rows // 4):
        for row_tap in range(3):
            first = 4 * pair + row_tap - 1
            upper = prev_ref[...] if first < 0 else image_ref[first]
            both = jnp.concatenate([upper, image_ref[first + 2]], axis=1)
            picked = dot_nn(both, pick).astype(BF)
            for col_tap in range(3):
                tap = 3 * row_tap + col_tap
                out_ref[tap * chans : (tap + 1) * chans, pair * width : (pair + 1) * width] = picked[
                    :, col_tap * width : (col_tap + 1) * width
                ]


def image_taps(image_in, prev_row):
    rows, chans, width = image_in.shape
    pixels = rows * width // 4
    return pl.pallas_call(
        taps_kernel,
        out_shape=jax.ShapeDtypeStruct((9 * chans, pixels), BF),
        compiler_params=params(60),
        cost_estimate=SMALL,
        name="taps",
    )(image_in, prev_row)


def grad_place(place_ref, flips, index):
    if not flips:
        return index
    return ((place_ref[1] + 8 - 2 * (index % 4)) & 7) ^ (index // 4)


def part_place(place_ref, flips, index):
    return place_ref[0] ^ index if flips else index


def interleave(width):
    place_in = iota((4 * width, 4 * width), 0)
    place_out = iota((4 * width, 4 * width), 1)
    return (
        ((place_in % (2 * width)) // width == place_out // (2 * width))
        & (2 * (place_in % width) + place_in // (2 * width) == place_out % (2 * width))
    ).astype(BF)


def image_kernel(
    grad_count, part_count, flips, width, place_ref, *refs
):
    grads, parts = refs[:grad_count], refs[grad_count : grad_count + part_count]
    out_ref, last_ref, edge_ref, grad_all, part_all, values, grad_sem, part_sem = refs[grad_count + part_count :]
    pixels, span = grads[0].shape
    outs, part_span = parts[0].shape
    chans = outs // 9
    pairs = pixels // (2 * width)
    tile = pixels

    def part_copy(index):
        start = pl.multiple_of(part_place(place_ref, flips, index) * part_span, part_span)
        return pltpu.make_async_copy(parts[index], part_all.at[:, pl.ds(start, part_span)], part_sem.at[index])

    def grad_copy(index):
        rows = grads[index].shape[0]
        start = pl.multiple_of(grad_place(place_ref, flips, min(index, grad_count - 2) if flips else index) * span, span)
        first = rows if flips and index == grad_count - 1 else 0
        return pltpu.make_async_copy(
            grads[index], grad_all.at[pl.ds(first, rows), pl.ds(start, span)], grad_sem.at[index]
        )

    for index in range(part_count):
        part_copy(index).start()
    for index in range(grad_count):
        grad_copy(index).start()

    lane = iota((chans, tile), 1)
    last_col = lane % width == width - 1
    row_end = lane >= tile - width
    place = interleave(width)

    def left(value):
        return jnp.where(last_col, 0.0, pltpu.roll(value, tile - 1, 1))

    def up_terms(terms):
        even, odd = terms[chans : 2 * chans], terms[2 * chans : 3 * chans] + left(terms[:chans])
        return pltpu.roll(even, tile - width, 1), pltpu.roll(odd, tile - width, 1)

    def tap_row(tap):
        return dot_nt(part_all[3 * tap * chans : 3 * (tap + 1) * chans], grad_all[...])

    third = lambda terms, index: terms[index * chans : (index + 1) * chans]
    for index in range(part_count):
        part_copy(index).wait()
    for index in range(grad_count):
        grad_copy(index).wait()
    upper = tap_row(0)
    own = up_terms(upper)
    middle = tap_row(1)
    lower = tap_row(2)
    phases = (
        (third(middle, 1), third(middle, 2) + left(third(middle, 0))),
        (
            third(lower, 1) + jnp.where(row_end, 0.0, own[0]),
            third(lower, 2) + left(third(lower, 0)) + jnp.where(row_end, 0.0, own[1]),
        ),
    )
    for index in range(2):
        at = slice(index * chans, (index + 1) * chans)
        edge_ref[at] = own[index][:, tile - 2 * width :]
        last_ref[at] = phases[1][index][:, tile - 2 * width :]
    for parity in range(2):
        even, odd = (value.astype(BF) for value in phases[parity])
        for pair in range(pairs):
            cols = slice(pair * 2 * width, (pair + 1) * 2 * width)
            at = slice((pairs * parity + pair) * chans, (pairs * parity + pair + 1) * chans)
            values[at, : 2 * width] = even[:, cols]
            values[at, 2 * width :] = odd[:, cols]
    placed = dot_nn(values[...], place).astype(BF)
    for parity in range(2):
        for pair in range(pairs):
            at = slice((pairs * parity + pair) * chans, (pairs * parity + pair + 1) * chans)
            first = 4 * pair + parity
            out_ref[first] = placed[at, : 2 * width]
            out_ref[first + 2] = placed[at, 2 * width :]


def image_gradient(place, flips, grads, parts, width):
    pixels, span = grads[0].shape
    outs, part_span = parts[0].shape
    full = part_span * len(parts)
    if flips:
        grads = [*grads[:-1], *grads[-1]]
    chans = outs // 9
    kernel = functools.partial(image_kernel, len(grads), len(parts), flips, width)
    anywhere = pl.BlockSpec(memory_space=pl.ANY)
    return pl.pallas_call(
        kernel,
        out_shape=(
            jax.ShapeDtypeStruct((2 * pixels // width, chans, 2 * width), BF),
            jax.ShapeDtypeStruct((2 * chans, 2 * width), F32),
            jax.ShapeDtypeStruct((2 * chans, 2 * width), F32),
        ),
        in_specs=[pl.BlockSpec(memory_space=pltpu.SMEM)] + [anywhere] * (len(grads) + len(parts)),
        out_specs=(pl.BlockSpec(memory_space=pltpu.VMEM),) * 3,
        scratch_shapes=[
            pltpu.VMEM((pixels, full), BF),
            pltpu.VMEM((outs, full), BF),
            pltpu.VMEM((pixels // width * chans, 4 * width), BF),
            pltpu.SemaphoreType.DMA((len(grads),)),
            pltpu.SemaphoreType.DMA((len(parts),)),
        ],
        compiler_params=params(60),
        cost_estimate=SMALL,
        name="image_grad",
    )(place, *grads, *parts)


def last_row(place_ref, last_ref, edge_ref, out_ref, row, sem):
    doubled, width = last_ref.shape
    chans, half = doubled // 2, width // 2
    inside = place_ref[0] % TILES != TILES - 1
    total = last_ref[...] + jnp.where((iota((doubled, width), 1) >= half) & inside, edge_ref[...], 0.0)
    both = jnp.concatenate([total[:chans], total[chans:]], axis=1).astype(BF)
    row[...] = dot_nn(both, interleave(half))[:, width:].astype(BF)
    copy = pltpu.make_async_copy(row, out_ref.at[out_ref.shape[0] - 1], sem)
    copy.start()
    return copy


def finish_kernel(place_ref, image_ref, last_ref, edge_ref, out_ref, row, sem):
    last_row(place_ref, last_ref, edge_ref, out_ref, row, sem).wait()


def finish_image(place, image, last, edge):
    anywhere, here = pl.BlockSpec(memory_space=pl.ANY), pl.BlockSpec(memory_space=pltpu.VMEM)
    return pl.pallas_call(
        finish_kernel,
        out_shape=jax.ShapeDtypeStruct(image.shape, BF),
        in_specs=[pl.BlockSpec(memory_space=pltpu.SMEM), anywhere, here, here],
        out_specs=anywhere,
        scratch_shapes=[pltpu.VMEM(image.shape[1:], BF), pltpu.SemaphoreType.DMA(())],
        input_output_aliases={1: 0},
        compiler_params=params(60),
        cost_estimate=SMALL,
        name="finish",
    )(place, image, last, edge)


def combine_kernel(scale, place_ref, image_ref, last_ref, edge_ref, *refs):
    refs, (image_out_ref, out_ref, row, sem, held, sums, in_sems, out_sems) = refs[:-8], refs[-8:]
    near_first, near_kept, near_got, far_kept, far_got, far_last, over_first, over_both, over_last = refs
    outs, span = near_first.shape
    rows = outs // CUTS
    core, outer, side = place_ref[0] & 1, place_ref[1] >> 1, place_ref[1] & 1
    step = (core + (outer & 1)) & 3
    mine = (((outer - step) & 3) >> 1) == (place_ref[0] >> 1)
    cases = (
        (mine, ((near_first, over_first), (far_kept, far_got, over_both))),
        (jnp.logical_not(mine), ((near_kept, near_got, over_both), (far_last, over_last))),
    )

    def load(ref, half, which, cut):
        return pltpu.make_async_copy(
            ref.at[pl.ds(cut * rows, rows)], held.at[half, which, cut], in_sems.at[half, which, cut]
        )

    def store(half, cut):
        start = pl.multiple_of((side if half == 0 else 1 - side) * span, span)
        return pltpu.make_async_copy(
            sums.at[half, cut], out_ref.at[pl.ds(cut * rows, rows), pl.ds(start, span)], out_sems.at[half, cut]
        )

    def case(halves):
        pieces = [(cut, half) for cut in range(CUTS) for half in range(2)]
        for cut, half in pieces:
            for which, ref in enumerate(halves[half]):
                load(ref, half, which, cut).start()
        row_copy = last_row(place_ref, last_ref, edge_ref, image_out_ref, row, sem)
        for cut, half in pieces:
            total = 0.0
            for which, ref in enumerate(halves[half]):
                load(ref, half, which, cut).wait()
                total = total + held[half, which, cut].astype(F32)
            sums[half, cut] = total * scale
            store(half, cut).start()
        row_copy.wait()

    for here, halves in cases:

        @pl.when(here)
        def _():
            case(halves)

    for cut in range(CUTS):
        for half in range(2):
            store(half, cut).wait()


def combine(place, image, last, edge, pieces, scale):
    anywhere, here = pl.BlockSpec(memory_space=pl.ANY), pl.BlockSpec(memory_space=pltpu.VMEM)
    outs, span = pieces[0].shape
    rows = outs // CUTS
    return pl.pallas_call(
        functools.partial(combine_kernel, scale),
        out_shape=(jax.ShapeDtypeStruct(image.shape, BF), jax.ShapeDtypeStruct((outs, 2 * span), F32)),
        in_specs=[pl.BlockSpec(memory_space=pltpu.SMEM), anywhere, here, here] + [anywhere] * len(pieces),
        out_specs=(anywhere, anywhere),
        scratch_shapes=[
            pltpu.VMEM(image.shape[1:], BF),
            pltpu.SemaphoreType.DMA(()),
            pltpu.VMEM((2, 3, CUTS, rows, span), BF),
            pltpu.VMEM((2, CUTS, rows, span), F32),
            pltpu.SemaphoreType.DMA((2, 3, CUTS)),
            pltpu.SemaphoreType.DMA((2, CUTS)),
        ],
        input_output_aliases={1: 0},
        compiler_params=params(60),
        cost_estimate=SMALL,
        name="combine",
    )(place, image, last, edge, *pieces)


def partial_kernel(count, split, chosen_blocks, place_ref, taps_ref, *refs):
    picks = len(chosen_blocks)
    core, turn = place_ref[0] & 1, (place_ref[1] >> 1) & 1
    whole = count - 1 if split else count
    inputs = whole + (2 if split else 0)
    blocks, outs = refs[:inputs], refs[inputs : inputs + picks]
    taps, grads, sums, grad_sems, taps_sems, out_sems = refs[inputs + picks :]
    half, span = taps_ref.shape[1] // 2, grads.shape[1] // picks
    rows = taps.shape[1]
    part = lambda ref, cut: ref.at[pl.ds(cut * rows, rows)]

    def chosen(pick, index):
        return pltpu.make_async_copy(blocks[index], grads.at[:, pl.ds(pick * span, span)], grad_sems.at[pick])

    def out_copy(pick, cut):
        return pltpu.make_async_copy(sums.at[pick, cut], part(outs[pick], cut), out_sems.at[pick, cut])

    taps_in = [pltpu.make_async_copy(part(taps_ref, cut), taps.at[cut], taps_sems.at[cut]) for cut in range(CUTS)]

    def start(pick):
        kept, phase, base = chosen_blocks[pick]
        step = base + ((2 * phase + (core if kept else 1 - core) + turn) & 3)
        for index in range(count):

            @pl.when(step == index)
            def _():
                if index < whole:
                    chosen(pick, index).start()
                else:
                    for piece in range(2):
                        pltpu.make_async_copy(
                            blocks[whole + piece],
                            grads.at[pl.ds(piece * half, half), pl.ds(pick * span, span)],
                            grad_sems.at[pick],
                        ).start()

    start(0)
    for copy in taps_in:
        copy.start()
    for pick in range(1, picks):
        start(pick)
    for first in range(0, picks, 2):
        for pick in (first, first + 1):
            chosen(pick, 0).wait()
        for cut in range(CUTS):
            if first == 0:
                taps_in[cut].wait()
            total = dot_nn(taps[cut], grads[:, first * span : (first + 2) * span]).astype(BF)
            for pick in (first, first + 1):
                sums[pick, cut] = total[:, (pick - first) * span : (pick - first + 1) * span]
                out_copy(pick, cut).start()
    for pick in range(picks):
        for cut in range(CUTS):
            out_copy(pick, cut).wait()


def kernel_partials(place, taps, blocks, chosen):
    outs, pixels = taps.shape
    span = blocks[0].shape[1]
    count, split = len(blocks), isinstance(blocks[-1], tuple)
    if split:
        blocks = [*blocks[:-1], *blocks[-1]]
    rows = outs // CUTS
    picks = len(chosen)
    anywhere = pl.BlockSpec(memory_space=pl.ANY)
    return pl.pallas_call(
        functools.partial(partial_kernel, count, split, tuple(chosen)),
        out_shape=(jax.ShapeDtypeStruct((outs, span), BF),) * picks,
        in_specs=[pl.BlockSpec(memory_space=pltpu.SMEM)] + [anywhere] * (1 + len(blocks)),
        out_specs=(anywhere,) * picks,
        scratch_shapes=[
            pltpu.VMEM((CUTS, rows, pixels), BF),
            pltpu.VMEM((pixels, picks * span), BF),
            pltpu.VMEM((picks, CUTS, rows, span), BF),
            pltpu.SemaphoreType.DMA((picks,)),
            pltpu.SemaphoreType.DMA((CUTS,)),
            pltpu.SemaphoreType.DMA((picks, CUTS)),
        ],
        compiler_params=params(60),
        cost_estimate=SMALL,
        name="partials",
    )(place, taps, *blocks)


def step_along(value, axis, steps):
    count = lax.axis_size(axis)
    return lax.ppermute(
        value, axis, [(source, source + steps) for source in range(count) if 0 <= source + steps < count]
    )


def swap(value, axis, bits):
    return lax.ppermute(value, axis, [(source, source ^ bits) for source in range(lax.axis_size(axis))])


def kernel_sum_plain(taps, grads):
    partial = jnp.concatenate([dot_nn(taps, grad).astype(BF) for grad in grads], axis=1)
    return lax.psum_scatter(partial, "pix", scatter_dimension=1, tiled=True).astype(F32)


def kept_step(core, outer, phase):
    return (2 * phase + core + outer % 2) % 4


def kept_here(pix, outer, phase):
    return (outer - kept_step(pix % 2, outer, phase)) % 4 // 2 == pix // 2


def send_over(value, phase):
    pairs = []
    for pix in range(4):
        for ch in range(8):
            if not kept_here(pix, ch // 2, phase):
                pairs.append((pix * 8 + ch, (pix ^ 2) * 8 + ch))
    return lax.ppermute(value, ("pix", "ch"), pairs)


def ring(value):
    return lax.ppermute(value, "ch", [(source, (source + 2) % 8) for source in range(8)])


def shards(image_in, pre_act, grad_out, conv_weight, mix_weight):
    tile_rows, width, chans = grad_out.shape
    in_chans = image_in.shape[1]
    pix_count, ch_count = lax.axis_size("pix"), lax.axis_size("ch")
    pix, ch = lax.axis_index("pix"), lax.axis_index("ch")
    first_tile = pix % TILES == 0
    pixels = tile_rows * width
    scale = 1.0 / float(pix_count * pixels) ** 0.5

    tie = lax.optimization_barrier
    place = jnp.stack([pix, ch]).astype(jnp.int32)
    prev_row = step_along(image_in[-1], "pix", 1)
    grad_pre, mix_part = pre_gradient(
        grad_out.reshape(pixels, chans),
        pre_act.reshape(pixels, chans),
        mix_weight.reshape(chans, GROUP_WIDTH),
    )
    kernel_own = conv_weight.reshape(9 * in_chans, -1)
    rings = pix_count == 4 and ch_count == 8
    taps = image_taps(image_in, jnp.where(first_tile, jnp.zeros_like(prev_row), prev_row))

    if rings:
        near, far = [grad_pre], [swap(grad_pre, "ch", 1)]
        near.append(ring(near[0]))
        mix_sum = mix_part + swap(mix_part, "pix", 2)
        grad_mix = (mix_sum + swap(mix_sum, "pix", 1)) * scale
        near[1], far[0], taps, grad_mix, kernel_own = tie((near[1], far[0], taps, grad_mix, kernel_own))
        far.append(swap(near[1], "ch", 1))
        near.append(ring(near[1]))
        kernel_x = swap(kernel_own, "pix", 2)
        kernel_core = swap(kernel_own, "pix", 1)
        near[2], far[1], kernel_core = tie((near[2], far[1], kernel_core))
        far.append(swap(near[2], "ch", 1))
        near.append(ring(near[2]))
        first = kernel_partials(place, taps, near[:3], [(0, 0, 0), (1, 0, 0)])
        near[3], far[2], first, kernel_x = tie((near[3], far[2], first, kernel_x))
        half = pixels // 2
        far.append((swap(near[3][:half], "ch", 1), ring(far[2][half:])))
        total_first = first[1] + swap(first[0], "pix", 1)
        kernel_xcore = swap(kernel_x, "pix", 1)
        second = kernel_partials(
            place, taps, near + far[:3], [(0, 0, 4), (0, 1, 0), (1, 0, 4), (1, 1, 0)]
        )
        far[3], total_first, second, kernel_xcore = tie((far[3], total_first, second, kernel_xcore))
        over_first = send_over(total_first, 0)
        got = [swap(second[0], "pix", 1), swap(second[1], "pix", 1)]
        mine = kept_here(pix, ch // 2, 0)
        crossing = jnp.where(mine, second[3], second[2]) + jnp.where(mine, got[1], got[0])
        third = kernel_partials(place, taps, far, [(0, 1, 0), (1, 1, 0)])
        third, over_first, crossing = tie((third, over_first, crossing))
        over_both = swap(crossing, "pix", 2)
        total_last = third[1] + swap(third[0], "pix", 1)
        over_last = send_over(total_last, 1)
        grads = near + far
        parts = [kernel_own, kernel_core, kernel_x, kernel_xcore]
        image_at = (place, total_last)
    else:
        grad_mix = lax.psum(mix_part, "pix") * scale
        grad_all = lax.all_gather(grad_pre, "ch", axis=0)
        kernel_all = lax.all_gather(kernel_own, "pix", axis=0)
        grads = [grad_all[index] for index in range(ch_count)]
        parts = [kernel_all[index] for index in range(pix_count)]
        grad_conv = kernel_sum_plain(taps, grads)
        image_at = (place,)
    grad_in, last, edge = image_gradient(tie(image_at)[0], rings, grads, parts, width)
    edge = step_along(edge, "pix", -1)
    if rings:
        grad_in, grad_conv = combine(
            place,
            grad_in,
            last,
            edge,
            [total_first, second[3], got[1], second[2], got[0], total_last, over_first, over_both, over_last],
            scale,
        )
    else:
        grad_in, grad_conv = finish_image(place, grad_in, last, edge), grad_conv * scale
    return (grad_in, grad_conv.reshape(conv_weight.shape), grad_mix.reshape(mix_weight.shape))


def solution(mesh):
    in_specs = (
        P("pix", "ch", None),
        P("pix", None, "ch"),
        P("pix", None, "ch"),
        P(None, None, "ch", "pix"),
        P("ch", None, None),
    )
    out_specs = (P("pix", "ch", None), P(None, None, "ch", "pix"), P("ch", None, None))
    return jax.shard_map(shards, mesh=mesh, in_specs=in_specs, out_specs=out_specs, check_vma=False)
```
